32 devices in a mesh: blk: 8 (over z, x), con: 4 (over y, core).
Axes of the slice: x: 2, y: 2, z: 4, core: 2. Of those that a mesh axis runs over, the one named last changes fastest.
Arguments:
- patch_rows: bfloat16 [4, 1536, 16, 1024], P('con', 'blk'), may hold values from -6 to 6
- subject_ids: int32 [1536], replicated, may hold values from 0 to 383
- logit_scale: float32 [2], replicated, may hold values from 5 to 20
- logit_bias: float32 [2], replicated, may hold values from -6 to -2
Outputs:
- grad_emb: float32 [4, 1536, 1024], P('con', 'blk')
The draws below stay inside these ranges and needn't reach their ends.
All inputs are finite; a program needn't handle non-finite values.
Results may differ from the reference program's by a relative error of at most 0.0037.
Values may be sent and summed in bfloat16 or wider, within the bound.
A program may use at most 128 MiB of HBM per device.

```python
import math
import jax
import jax.numpy as jnp
from jax import lax

D = 1024
PATCHES = 16
B = 1536
CONTRASTS = 4
PAIRS = 2


def place_ends(result, rng, least, largest):
    index_at = [jax.random.randint(jax.random.fold_in(rng, axis), (), 0, length) for axis, length in enumerate(result.shape)]
    main_axis = result.shape.index(max(result.shape))
    next_to = index_at[:main_axis] + [(index_at[main_axis] + 1) % result.shape[main_axis]] + index_at[main_axis + 1:]
    return result.at[tuple(index_at)].set(least).at[tuple(next_to)].set(largest)


def level_of(key, shape, split, least, top_value):
    level = 1.0
    for position, blocks in split:
        draws = jax.random.uniform(jax.random.fold_in(jax.random.fold_in(key, 6), position), (blocks,), jnp.float32, least / len(split), top_value / len(split))
        level = level * jnp.repeat(jnp.exp(draws), shape[position] // blocks).reshape((-1,) + (1,) * (len(shape) - 1 - position))
    return level


def normal_values(stream_key, dims, deviation, bound, cuts=(), kind=jnp.bfloat16):
    entries = deviation * jax.random.normal(stream_key, dims, jnp.float32)
    if cuts:
        entries = entries * level_of(stream_key, dims, cuts, -0.22, 0.18)
    return jnp.clip(entries, -bound, bound).astype(kind)


def setup_inputs(seed: int = 0) -> dict:
    keys = jax.random.split(jax.random.key(seed), 5)
    return {
        "patch_rows": normal_values(keys[0], (CONTRASTS, B, PATCHES, D), 1.0, 6.0, ((0, 4), (1, 8))),
        "subject_ids": place_ends(jax.random.randint(keys[1], (B,), 0, B // 4), jax.random.fold_in(keys[1], 1), 0, (B // 4) - 1).astype(jnp.int32),
        "logit_scale": jnp.clip(jnp.exp(jax.random.uniform(keys[2], (PAIRS,), jnp.float32, math.log(5.0), math.log(20.0))), 5.0, 20.0),
        "logit_bias": jnp.clip(jax.random.uniform(keys[3], (PAIRS,), jnp.float32, -6.0, -2.0), -6.0, -2.0),
    }


def pair_grads(first_emb, second_emb, subject_ids, scale_value, bias_value):
    block = math.gcd(B, 512)

    def scan_rows(grad_second, block_index):
        first_row = (block_index * block).astype(jnp.int32)
        first_block = lax.dynamic_slice_in_dim(first_emb, first_row, block, 0)
        block_ids = lax.dynamic_slice_in_dim(subject_ids, first_row, block, 0)
        logits = scale_value * lax.dot_general(first_block, second_emb, (((1,), (1,)), ((), ())), preferred_element_type=jnp.float32) + bias_value
        label_sign = jnp.where(block_ids[:, None] == subject_ids[None, :], 1.0, -1.0).astype(jnp.float32)
        coeff = (scale_value * (jax.nn.sigmoid(label_sign * logits) - 1.0) * label_sign).astype(jnp.bfloat16)
        grad_block = jnp.dot(coeff, second_emb, preferred_element_type=jnp.float32)
        grad_second = grad_second + lax.dot_general(coeff, first_block, (((0,), (0,)), ((), ())), preferred_element_type=jnp.float32)
        return (grad_second, grad_block)
    grad_second, grad_blocks = lax.scan(scan_rows, jnp.zeros((B, D), jnp.float32), jnp.arange(B // block).astype(jnp.int32))
    return (grad_blocks.reshape(B, D), grad_second)

def reference(patch_rows, subject_ids, logit_scale, logit_bias):
    pooled = lax.optimization_barrier(jnp.sum(patch_rows, axis=2, dtype=jnp.float32)) / PATCHES
    row_norms = jnp.sqrt(lax.optimization_barrier(jnp.sum(pooled * pooled, axis=2, keepdims=True)) + 1e-06)
    emb = (pooled / row_norms).astype(jnp.bfloat16)
    results = []
    for pair_index in range(PAIRS):
        grad_first, grad_second = pair_grads(emb[2 * pair_index], emb[2 * pair_index + 1], subject_ids, logit_scale[pair_index], logit_bias[pair_index])
        results.append(grad_first)
        results.append(grad_second)
    return jnp.stack(results, axis=0)
```

```python
import functools
import jax
import jax.numpy as jnp
from jax import lax
from jax.experimental import pallas as pl
from jax.experimental.pallas import tpu as pltpu
from jax.sharding import PartitionSpec as P

MESH = pl.DeviceIdType.MESH


def kernel(n, fast, scale_ref, bias_ref, ids_ref, x_ref, out_ref, xbuf, own, blocks, ids_col,
           in_sem, swap_sem, recv_sem, up_sem, down_sem, cross_sem):
    rows, patches, width = x_ref.shape[1:]
    slow = n // fast
    con = lax.axis_index("con")
    pos = lax.axis_index("blk")
    z = pos // fast
    x = pos % fast
    pair = con // 2
    partner = con + 1 - 2 * (con % 2)
    across = x + 1 - 2 * (x % 2)
    group = 16
    steps = xbuf.shape[0]
    chunk = rows // steps

    def load(i):
        return pltpu.make_async_copy(
            x_ref.at[0, pl.ds(i * chunk, chunk)], xbuf.at[i], in_sem.at[i])

    for i in range(steps):
        load(i).start()

    barrier = pltpu.get_barrier_semaphore()
    pl.semaphore_signal(barrier, inc=1, device_id=(pos, partner), device_id_type=MESH)
    pl.semaphore_signal(barrier, inc=1, device_id=(z * fast + across, con), device_id_type=MESH)

    @pl.when(z > 0)
    def _():
        pl.semaphore_signal(barrier, inc=1, device_id=(pos - fast, con), device_id_type=MESH)

    @pl.when(z < slow - 1)
    def _():
        pl.semaphore_signal(barrier, inc=1, device_id=(pos + fast, con), device_id_type=MESH)

    mine = ids_ref[pl.ds(pos, 1), :].astype(jnp.float32)
    eye = (lax.broadcasted_iota(jnp.int32, (rows, rows), 0)
           == lax.broadcasted_iota(jnp.int32, (rows, rows), 1))
    ids_col[...] = jnp.sum(jnp.where(eye, mine, 0.0), axis=1, keepdims=True)

    ones = (lax.broadcasted_iota(jnp.int32, (group, group * patches), 1) // patches
            == lax.broadcasted_iota(jnp.int32, (group, group * patches), 0)).astype(jnp.bfloat16)
    for i in range(steps):
        load(i).wait()
        for g in range(chunk // group):
            tile = xbuf[i, pl.ds(g * group, group)].reshape(group * patches, width)
            pooled = jnp.dot(ones, tile, preferred_element_type=jnp.float32) * (1.0 / patches)
            norm = lax.rsqrt(jnp.sum(pooled * pooled, axis=1, keepdims=True) + 1e-6)
            own[pl.ds(i * chunk + g * group, group), :] = (pooled * norm).astype(jnp.bfloat16)

    pl.semaphore_wait(barrier, 2 + jnp.where(z > 0, 1, 0) + jnp.where(z < slow - 1, 1, 0))

    swap = pltpu.make_async_remote_copy(
        src_ref=own, dst_ref=blocks.at[pos], send_sem=swap_sem, recv_sem=recv_sem.at[pos],
        device_id=(pos, partner), device_id_type=MESH)
    swap.start()

    def send(slot, target, sem):
        return pltpu.make_async_remote_copy(
            src_ref=blocks.at[slot], dst_ref=blocks.at[slot], send_sem=sem.at[slot // fast],
            recv_sem=recv_sem.at[slot], device_id=(target, con), device_id_type=MESH)

    def arrived(slot):
        pltpu.make_async_remote_copy(
            src_ref=blocks.at[slot], dst_ref=blocks.at[slot], send_sem=swap_sem,
            recv_sem=recv_sem.at[slot], device_id=(pos, partner), device_id_type=MESH).wait_recv()

    near = jnp.minimum(z, slow - 1 - z)
    far_sign = jnp.where(z < slow - 1 - z, 1, -1)

    def layer(k):
        both = ((k + 1) // 2) * jnp.where(k % 2 == 1, 1, -1)
        return z + jnp.where(k <= 2 * near, both, far_sign * (k - near))

    scale = scale_ref[pair]
    bias = bias_ref[pair]

    def add_block(slot, first):
        block = blocks[slot]
        dots = lax.dot_general(own[...], block, (((1,), (1,)), ((), ())),
                               preferred_element_type=jnp.float32)
        logits = scale * dots + bias
        same = ids_col[...] == ids_ref[pl.ds(slot, 1), :].astype(jnp.float32)
        sign = jnp.where(same, 1.0, -1.0)
        coeff = ((-scale * sign) / (1.0 + jnp.exp(sign * logits))).astype(jnp.bfloat16)
        grad = jnp.dot(coeff, block, preferred_element_type=jnp.float32)
        if first:
            out_ref[0] = grad
        else:
            out_ref[0] += grad

    def relay(k):
        zz = layer(k)
        slot = zz * fast + x
        arrived(slot)

        @pl.when((z < slow - 1) & (zz <= z))
        def _():
            send(slot, pos + fast, up_sem).start()

        @pl.when((z > 0) & (zz >= z))
        def _():
            send(slot, pos - fast, down_sem).start()

        send(slot, z * fast + across, cross_sem).start()
        return slot

    add_block(relay(0), True)

    def own_line(k, carry):
        add_block(relay(k), False)
        return carry

    lax.fori_loop(1, slow, own_line, 0)

    def other_line(k, carry):
        slot = layer(k) * fast + across
        arrived(slot)
        add_block(slot, False)
        return carry

    lax.fori_loop(0, slow, other_line, 0)

    swap.wait_send()

    def drain(zz, carry):
        slot = zz * fast + x

        @pl.when((z < slow - 1) & (zz <= z))
        def _():
            send(slot, pos + fast, up_sem).wait_send()

        @pl.when((z > 0) & (zz >= z))
        def _():
            send(slot, pos - fast, down_sem).wait_send()

        send(slot, z * fast + across, cross_sem).wait_send()
        return carry

    lax.fori_loop(0, slow, drain, 0)


def solution(mesh):
    n = mesh.shape["blk"]
    fast = 2
    slow = n // fast

    def on_device(patch_rows, subject_ids, logit_scale, logit_bias):
        _, rows, patches, width = patch_rows.shape
        chunk = 48 if rows % 48 == 0 else rows
        return pl.pallas_call(
            functools.partial(kernel, n, fast),
            out_shape=jax.ShapeDtypeStruct((1, rows, width), jnp.float32),
            in_specs=[pl.BlockSpec(memory_space=pltpu.SMEM), pl.BlockSpec(memory_space=pltpu.SMEM),
                      pl.BlockSpec(memory_space=pltpu.VMEM), pl.BlockSpec(memory_space=pl.ANY)],
            out_specs=pl.BlockSpec(memory_space=pltpu.VMEM),
            scratch_shapes=[
                pltpu.VMEM((rows // chunk, chunk, patches, width), jnp.bfloat16),
                pltpu.VMEM((rows, width), jnp.bfloat16),
                pltpu.VMEM((n, rows, width), jnp.bfloat16),
                pltpu.VMEM((rows, 1), jnp.float32),
                pltpu.SemaphoreType.DMA((rows // chunk,)),
                pltpu.SemaphoreType.DMA,
                pltpu.SemaphoreType.DMA((n,)),
                pltpu.SemaphoreType.DMA((slow,)),
                pltpu.SemaphoreType.DMA((slow,)),
                pltpu.SemaphoreType.DMA((slow,)),
            ],
            compiler_params=pltpu.CompilerParams(
                collective_id=0, has_side_effects=True, vmem_limit_bytes=52 * 2**20),
        )(logit_scale, logit_bias, subject_ids.reshape(n, rows), patch_rows)

    return jax.shard_map(
        on_device, mesh=mesh, in_specs=(P("con", "blk", None, None), P(), P(), P()),
        out_specs=P("con", "blk", None), check_vma=False)
```

```python
import functools
import jax
import jax.numpy as jnp
from jax import lax
from jax.experimental import pallas as pl
from jax.experimental.pallas import tpu as pltpu
from jax.sharding import PartitionSpec as P

MESH = pl.DeviceIdType.MESH


def kernel(n, fast, scale_ref, bias_ref, ids_ref, x_ref, out_ref, xbuf, own, a_rows, b_rows,
           ids_col, part, acc_b, rs_out, rs_up, rs_down, b_half_out, b_half_in, b_cross_out,
           b_cross_in, last_out, last_in, in_sem, swap_send, swap_recv, a_recv, up_send, down_send,
           b_cross_send, b_cross_recv, b_relay_send, b_relay_recv, rs_send, up_recv, down_recv,
           gb_send, gb_recv):
    rows, patches, width = x_ref.shape[1:]
    half = rows // 2
    slow = n // fast
    con = lax.axis_index("con")
    pos = lax.axis_index("blk")
    z = pos // fast
    x = pos % fast
    pair = con // 2
    core = con % 2
    partner = con + 1 - 2 * core
    across = x + 1 - 2 * (x % 2)
    group = 16
    steps = xbuf.shape[0]
    chunk = rows // steps
    on_chip = dict(device_id=(pos, partner), device_id_type=MESH)
    on_cross = dict(device_id=(z * fast + across, con), device_id_type=MESH)
    on_up = dict(device_id=(pos + fast, con), device_id_type=MESH)
    on_down = dict(device_id=(pos - fast, con), device_id_type=MESH)
    has_up = z < slow - 1
    has_down = z > 0

    def load(i):
        return pltpu.make_async_copy(
            x_ref.at[0, pl.ds(i * chunk, chunk)], xbuf.at[i], in_sem.at[i])

    for i in range(steps):
        load(i).start()

    barrier = pltpu.get_barrier_semaphore()
    pl.semaphore_signal(barrier, inc=1, **on_chip)
    pl.semaphore_signal(barrier, inc=1, **on_cross)

    @pl.when(has_down)
    def _():
        pl.semaphore_signal(barrier, inc=1, **on_down)

    @pl.when(has_up)
    def _():
        pl.semaphore_signal(barrier, inc=1, **on_up)

    eye = (lax.broadcasted_iota(jnp.int32, (rows, rows), 0)
           == lax.broadcasted_iota(jnp.int32, (rows, rows), 1))

    def column(zz, carry):
        line = ids_ref[pl.ds(zz * fast + x, 1), :].astype(jnp.float32)
        ids_col[zz] = jnp.sum(jnp.where(eye, line, 0.0), axis=1, keepdims=True)
        return carry

    lax.fori_loop(0, slow, column, 0)

    ones = (lax.broadcasted_iota(jnp.int32, (group, group * patches), 1) // patches
            == lax.broadcasted_iota(jnp.int32, (group, group * patches), 0)).astype(jnp.bfloat16)
    for i in range(steps):
        load(i).wait()
        for g in range(chunk // group):
            tile = xbuf[i, pl.ds(g * group, group)].reshape(group * patches, width)
            pooled = jnp.dot(ones, tile, preferred_element_type=jnp.float32) * (1.0 / patches)
            norm = lax.rsqrt(jnp.sum(pooled * pooled, axis=1, keepdims=True) + 1e-6)
            at = i * chunk + g * group
            own[at // half, pl.ds(at % half, group), :] = (pooled * norm).astype(jnp.bfloat16)

    pl.semaphore_wait(barrier, 2 + jnp.where(has_down, 1, 0) + jnp.where(has_up, 1, 0))

    a_swap = pltpu.make_async_remote_copy(
        src_ref=own.at[1], dst_ref=a_rows.at[z], send_sem=swap_send, recv_sem=a_recv.at[z], **on_chip)
    b_swap = pltpu.make_async_remote_copy(
        src_ref=own, dst_ref=b_rows.at[x], send_sem=swap_send, recv_sem=swap_recv, **on_chip)
    b_cross = pltpu.make_async_remote_copy(
        src_ref=b_rows.at[x, core], dst_ref=b_rows.at[x, core], send_sem=b_cross_send,
        recv_sem=b_cross_recv, **on_cross)
    b_cross_arrival = pltpu.make_async_remote_copy(
        src_ref=b_rows.at[across, core], dst_ref=b_rows.at[across, core], send_sem=b_cross_send,
        recv_sem=b_cross_recv, **on_cross)
    b_relay = pltpu.make_async_remote_copy(
        src_ref=b_rows.at[across, core], dst_ref=b_rows.at[across, core], send_sem=b_relay_send,
        recv_sem=b_relay_recv, **on_chip)
    b_relay_arrival = pltpu.make_async_remote_copy(
        src_ref=b_rows.at[across, 1 - core], dst_ref=b_rows.at[across, 1 - core],
        send_sem=b_relay_send, recv_sem=b_relay_recv, **on_chip)

    def a_up(zz):
        return pltpu.make_async_remote_copy(
            src_ref=a_rows.at[zz], dst_ref=a_rows.at[zz], send_sem=up_send.at[zz],
            recv_sem=a_recv.at[zz], **on_up)

    def a_down(zz):
        return pltpu.make_async_remote_copy(
            src_ref=a_rows.at[zz], dst_ref=a_rows.at[zz], send_sem=down_send.at[zz],
            recv_sem=a_recv.at[zz], **on_down)

    def forward(zz):
        @pl.when(has_up & (zz <= z))
        def _():
            a_up(zz).start()

        @pl.when(has_down & (zz >= z))
        def _():
            a_down(zz).start()

    @pl.when(core == 0)
    def _():
        a_rows[z] = own[0]
        a_swap.start()
        forward(z)
        b_swap.wait_recv()
        b_cross.start()

    @pl.when(core == 1)
    def _():
        b_rows[x] = own[...]
        b_swap.start()
        b_cross.start()
        a_swap.wait_recv()
        forward(z)

    near = jnp.minimum(z, slow - 1 - z)
    far_sign = jnp.where(z < slow - 1 - z, 1, -1)

    def layer(k):
        both = ((k + 1) // 2) * jnp.where(k % 2 == 1, 1, -1)
        return z + jnp.where(k <= 2 * near, both, far_sign * (k - near))

    scale = scale_ref[pair]
    bias = bias_ref[pair]

    def block(zz, xx, first):
        rows_a = a_rows[zz]
        rows_b = b_rows[xx].reshape(rows, width)
        dots = lax.dot_general(rows_a, rows_b, (((1,), (1,)), ((), ())),
                               preferred_element_type=jnp.float32)
        logits = scale * dots + bias
        labels = ids_col[zz, pl.ds(pl.multiple_of(core * half, 16), half), :]
        same = labels == ids_ref[pl.ds(z * fast + xx, 1), :].astype(jnp.float32)
        sign = jnp.where(same, 1.0, -1.0)
        coeff = ((-scale * sign) / (1.0 + jnp.exp(sign * logits))).astype(jnp.bfloat16)
        grad_b = lax.dot_general(coeff, rows_a, (((0,), (0,)), ((), ())),
                                 preferred_element_type=jnp.float32).reshape(2, half, width)
        if first:
            acc_b[xx] = grad_b
        else:
            acc_b[xx] += grad_b
        return jnp.dot(coeff, rows_b, preferred_element_type=jnp.float32)

    def rs_to_up(d):
        return pltpu.make_async_remote_copy(
            src_ref=rs_out.at[d], dst_ref=rs_up.at[d], send_sem=rs_send.at[d],
            recv_sem=up_recv.at[d], **on_up)

    def rs_to_down(d):
        return pltpu.make_async_remote_copy(
            src_ref=rs_out.at[d], dst_ref=rs_down.at[d], send_sem=rs_send.at[d],
            recv_sem=down_recv.at[d], **on_down)

    def compute(zz):
        part[zz] = block(zz, x, False)
        part[zz] += block(zz, across, False)

        @pl.when((z == 0) & (zz > z))
        def _():
            rs_out[zz] = part[zz].astype(jnp.bfloat16)
            rs_to_up(zz).start()

        @pl.when((z == slow - 1) & (zz < z))
        def _():
            rs_out[zz] = part[zz].astype(jnp.bfloat16)
            rs_to_down(zz).start()

    def relay(k):
        zz = layer(k)
        a_up(zz).wait_recv()
        forward(zz)
        return zz

    part[z] = block(z, x, True)
    if slow > 1:
        second = relay(1)
    b_cross_arrival.wait_recv()
    b_relay.start()
    b_relay_arrival.wait_recv()
    part[z] += block(z, across, True)
    if slow > 1:
        compute(second)

    def line(k, carry):
        compute(relay(k))
        return carry

    lax.fori_loop(2, slow, line, 0)

    b_half = pltpu.make_async_remote_copy(
        src_ref=b_half_out, dst_ref=b_half_in, send_sem=gb_send.at[0], recv_sem=gb_recv.at[0], **on_chip)
    b_sum = pltpu.make_async_remote_copy(
        src_ref=b_cross_out, dst_ref=b_cross_in, send_sem=gb_send.at[1], recv_sem=gb_recv.at[1], **on_cross)
    b_half_out[...] = acc_b[across, 1 - core].astype(jnp.bfloat16)
    b_half.start()
    b_half.wait_recv()
    b_cross_out[...] = (acc_b[across, core] + b_half_in[...].astype(jnp.float32)).astype(jnp.bfloat16)
    b_sum.start()

    def pass_on(t, carry):
        @pl.when(has_down & (t > 2 * z) & (t < slow + z))
        def _():
            d = t - z
            rs_to_up(d).wait_recv()
            rs_out[d] = (part[d] + rs_up[d].astype(jnp.float32)).astype(jnp.bfloat16)
            rs_to_up(d).start()

        z_back = slow - 1 - z

        @pl.when(has_up & (t > 2 * z_back) & (t < slow + z_back))
        def _():
            d = slow - 1 - (t - z_back)
            rs_to_down(d).wait_recv()
            rs_out[d] = (part[d] + rs_down[d].astype(jnp.float32)).astype(jnp.bfloat16)
            rs_to_down(d).start()

        return carry

    lax.fori_loop(3, 2 * slow - 2, pass_on, 0)

    b_sum.wait_recv()
    to_b = pltpu.make_async_remote_copy(
        src_ref=last_out, dst_ref=last_in, send_sem=gb_send.at[2], recv_sem=gb_recv.at[2], **on_chip)
    to_a = pltpu.make_async_remote_copy(
        src_ref=last_out.at[0], dst_ref=last_in.at[0], send_sem=gb_send.at[2], recv_sem=gb_recv.at[2],
        **on_chip)

    @pl.when(core == 0)
    def _():
        last_out[0] = (acc_b[x, 0] + b_cross_in[...].astype(jnp.float32)).astype(jnp.bfloat16)
        last_out[1] = acc_b[x, 1].astype(jnp.bfloat16)
        to_b.start()

    @pl.when(has_down)
    def _():
        rs_to_up(z).wait_recv()
        part[z] += rs_up[z].astype(jnp.float32)

    @pl.when(has_up)
    def _():
        rs_to_down(z).wait_recv()
        part[z] += rs_down[z].astype(jnp.float32)

    @pl.when(core == 0)
    def _():
        out_ref[0, pl.ds(0, half), :] = part[z]
        to_a.wait_recv()
        out_ref[0, pl.ds(half, half), :] = last_in[0].astype(jnp.float32)
        a_swap.wait_send()
        to_b.wait_send()

    @pl.when(core == 1)
    def _():
        last_out[0] = part[z].astype(jnp.bfloat16)
        to_a.start()
        to_b.wait_recv()
        out_ref[0, pl.ds(0, half), :] = acc_b[x, 0] + last_in[0].astype(jnp.float32)
        out_ref[0, pl.ds(half, half), :] = (
            acc_b[x, 1] + last_in[1].astype(jnp.float32) + b_cross_in[...].astype(jnp.float32))
        b_swap.wait_send()
        to_a.wait_send()

    b_cross.wait_send()
    b_relay.wait_send()
    b_half.wait_send()
    b_sum.wait_send()

    def drain(zz, carry):
        @pl.when(has_up & (zz <= z))
        def _():
            a_up(zz).wait_send()

        @pl.when(has_down & (zz >= z))
        def _():
            a_down(zz).wait_send()

        @pl.when(zz > z)
        def _():
            rs_to_up(zz).wait_send()

        @pl.when(zz < z)
        def _():
            rs_to_down(zz).wait_send()

        return carry

    lax.fori_loop(0, slow, drain, 0)


def solution(mesh):
    n = mesh.shape["blk"]
    fast = 2
    slow = n // fast

    def on_device(patch_rows, subject_ids, logit_scale, logit_bias):
        _, rows, patches, width = patch_rows.shape
        half = rows // 2
        chunk = 48 if rows % 48 == 0 else rows
        bf16, f32 = jnp.bfloat16, jnp.float32
        dma = pltpu.SemaphoreType.DMA
        return pl.pallas_call(
            functools.partial(kernel, n, fast),
            out_shape=jax.ShapeDtypeStruct((1, rows, width), jnp.float32),
            in_specs=[pl.BlockSpec(memory_space=pltpu.SMEM), pl.BlockSpec(memory_space=pltpu.SMEM),
                      pl.BlockSpec(memory_space=pltpu.VMEM), pl.BlockSpec(memory_space=pl.ANY)],
            out_specs=pl.BlockSpec(memory_space=pltpu.VMEM),
            scratch_shapes=[
                pltpu.VMEM((rows // chunk, chunk, patches, width), bf16),
                pltpu.VMEM((2, half, width), bf16),
                pltpu.VMEM((slow, half, width), bf16),
                pltpu.VMEM((fast, 2, half, width), bf16),
                pltpu.VMEM((slow, rows, 1), f32),
                pltpu.VMEM((slow, half, width), f32),
                pltpu.VMEM((fast, 2, half, width), f32),
                pltpu.VMEM((slow, half, width), bf16),
                pltpu.VMEM((slow, half, width), bf16),
                pltpu.VMEM((slow, half, width), bf16),
                pltpu.VMEM((half, width), bf16),
                pltpu.VMEM((half, width), bf16),
                pltpu.VMEM((half, width), bf16),
                pltpu.VMEM((half, width), bf16),
                pltpu.VMEM((2, half, width), bf16),
                pltpu.VMEM((2, half, width), bf16),
                dma((rows // chunk,)), dma, dma, dma((slow,)), dma((slow,)), dma((slow,)),
                dma, dma, dma, dma, dma((slow,)), dma((slow,)), dma((slow,)), dma((3,)), dma((3,)),
            ],
            compiler_params=pltpu.CompilerParams(
                collective_id=0, has_side_effects=True, vmem_limit_bytes=60 * 2**20),
        )(logit_scale, logit_bias, subject_ids.reshape(n, rows), patch_rows)

    return jax.shard_map(
        on_device, mesh=mesh, in_specs=(P("con", "blk", None, None), P(), P(), P()),
        out_specs=P("con", "blk", None), check_vma=False)
```

```python
import functools
import jax
import jax.numpy as jnp
from jax import lax
from jax.experimental import pallas as pl
from jax.experimental.pallas import tpu as pltpu
from jax.sharding import PartitionSpec as P

MESH = pl.DeviceIdType.MESH


def kernel(n, fast, scale_ref, bias_ref, ids_ref, x_ref, out_ref, xbuf, own, a_rows, b_rows,
           ids_col, part, acc_b, rs_out, rs_up, rs_down, b_half_out, b_half_in, b_cross_out,
           b_cross_in, last_out, last_in, in_sem, swap_send, swap_recv, a_recv, up_send, down_send,
           b_cross_send, b_cross_recv, b_relay_send, b_relay_recv, rs_send, up_recv, down_recv,
           gb_send, gb_recv):
    rows, patches, width = x_ref.shape[1:]
    half = rows // 2
    slow = n // fast
    con = lax.axis_index("con")
    pos = lax.axis_index("blk")
    z = pos // fast
    x = pos % fast
    pair = con // 2
    core = con % 2
    partner = con + 1 - 2 * core
    across = x + 1 - 2 * (x % 2)
    group = 16
    steps = xbuf.shape[0]
    chunk = rows // steps
    on_chip = dict(device_id=(pos, partner), device_id_type=MESH)
    on_cross = dict(device_id=(z * fast + across, con), device_id_type=MESH)
    on_up = dict(device_id=(pos + fast, con), device_id_type=MESH)
    on_down = dict(device_id=(pos - fast, con), device_id_type=MESH)
    has_up = z < slow - 1
    has_down = z > 0

    def load(i):
        return pltpu.make_async_copy(
            x_ref.at[0, pl.ds(i * chunk, chunk)], xbuf.at[i], in_sem.at[i])

    for i in range(steps):
        load(i).start()

    barrier = pltpu.get_barrier_semaphore()
    pl.semaphore_signal(barrier, inc=1, **on_chip)
    pl.semaphore_signal(barrier, inc=1, **on_cross)

    @pl.when(has_down)
    def _():
        pl.semaphore_signal(barrier, inc=1, **on_down)

    @pl.when(has_up)
    def _():
        pl.semaphore_signal(barrier, inc=1, **on_up)

    eye = (lax.broadcasted_iota(jnp.int32, (rows, rows), 0)
           == lax.broadcasted_iota(jnp.int32, (rows, rows), 1))

    def column(zz, carry):
        line = ids_ref[pl.ds(zz * fast + x, 1), :].astype(jnp.float32)
        ids_col[zz] = jnp.sum(jnp.where(eye, line, 0.0), axis=1, keepdims=True)
        return carry

    lax.fori_loop(0, slow, column, 0)

    ones = (lax.broadcasted_iota(jnp.int32, (group, group * patches), 1) // patches
            == lax.broadcasted_iota(jnp.int32, (group, group * patches), 0)).astype(jnp.bfloat16)
    for i in range(steps):
        load(i).wait()
        for g in range(chunk // group):
            tile = xbuf[i, pl.ds(g * group, group)].reshape(group * patches, width)
            pooled = jnp.dot(ones, tile, preferred_element_type=jnp.float32) * (1.0 / patches)
            norm = lax.rsqrt(jnp.sum(pooled * pooled, axis=1, keepdims=True) + 1e-6)
            at = i * chunk + g * group
            own[at // half, pl.ds(at % half, group), :] = (pooled * norm).astype(jnp.bfloat16)

    pl.semaphore_wait(barrier, 2 + jnp.where(has_down, 1, 0) + jnp.where(has_up, 1, 0))

    a_swap = pltpu.make_async_remote_copy(
        src_ref=own.at[1], dst_ref=a_rows.at[z], send_sem=swap_send, recv_sem=a_recv.at[z], **on_chip)
    b_swap = pltpu.make_async_remote_copy(
        src_ref=own, dst_ref=b_rows.at[x], send_sem=swap_send, recv_sem=swap_recv, **on_chip)
    b_cross = pltpu.make_async_remote_copy(
        src_ref=b_rows.at[x, core], dst_ref=b_rows.at[x, core], send_sem=b_cross_send,
        recv_sem=b_cross_recv, **on_cross)
    b_cross_arrival = pltpu.make_async_remote_copy(
        src_ref=b_rows.at[across, core], dst_ref=b_rows.at[across, core], send_sem=b_cross_send,
        recv_sem=b_cross_recv, **on_cross)
    b_relay = pltpu.make_async_remote_copy(
        src_ref=b_rows.at[across, core], dst_ref=b_rows.at[across, core], send_sem=b_relay_send,
        recv_sem=b_relay_recv, **on_chip)
    b_relay_arrival = pltpu.make_async_remote_copy(
        src_ref=b_rows.at[across, 1 - core], dst_ref=b_rows.at[across, 1 - core],
        send_sem=b_relay_send, recv_sem=b_relay_recv, **on_chip)

    def a_up(zz):
        return pltpu.make_async_remote_copy(
            src_ref=a_rows.at[zz], dst_ref=a_rows.at[zz], send_sem=up_send.at[zz],
            recv_sem=a_recv.at[zz], **on_up)

    def a_down(zz):
        return pltpu.make_async_remote_copy(
            src_ref=a_rows.at[zz], dst_ref=a_rows.at[zz], send_sem=down_send.at[zz],
            recv_sem=a_recv.at[zz], **on_down)

    def forward(zz):
        @pl.when(has_up & (zz <= z))
        def _():
            a_up(zz).start()

        @pl.when(has_down & (zz >= z))
        def _():
            a_down(zz).start()

    @pl.when(core == 0)
    def _():
        a_rows[z] = own[0]
        a_swap.start()
        forward(z)
        b_swap.wait_recv()
        b_cross.start()

    @pl.when(core == 1)
    def _():
        b_rows[x] = own[...]
        b_swap.start()
        b_cross.start()
        a_swap.wait_recv()
        forward(z)

    near = jnp.minimum(z, slow - 1 - z)
    far_sign = jnp.where(z < slow - 1 - z, 1, -1)

    def layer(k):
        both = ((k + 1) // 2) * jnp.where(k % 2 == 1, 1, -1)
        return z + jnp.where(k <= 2 * near, both, far_sign * (k - near))

    scale = scale_ref[pair]
    bias = bias_ref[pair]

    def block(zz, xx, first):
        rows_a = a_rows[zz]
        rows_b = b_rows[xx].reshape(rows, width)
        dots = lax.dot_general(rows_a, rows_b, (((1,), (1,)), ((), ())),
                               preferred_element_type=jnp.float32)
        logits = scale * dots + bias
        labels = ids_col[zz, pl.ds(pl.multiple_of(core * half, 16), half), :]
        same = labels == ids_ref[pl.ds(z * fast + xx, 1), :].astype(jnp.float32)
        sign = jnp.where(same, 1.0, -1.0)
        coeff = ((-scale * sign) / (1.0 + jnp.exp(sign * logits))).astype(jnp.bfloat16)
        grad_b = lax.dot_general(coeff, rows_a, (((0,), (0,)), ((), ())),
                                 preferred_element_type=jnp.float32).reshape(2, half, width)
        if first:
            acc_b[xx] = grad_b
        else:
            acc_b[xx] += grad_b
        return jnp.dot(coeff, rows_b, preferred_element_type=jnp.float32)

    def rs_to_up(d):
        return pltpu.make_async_remote_copy(
            src_ref=rs_out.at[d], dst_ref=rs_up.at[d], send_sem=rs_send.at[d],
            recv_sem=up_recv.at[d], **on_up)

    def rs_to_down(d):
        return pltpu.make_async_remote_copy(
            src_ref=rs_out.at[d], dst_ref=rs_down.at[d], send_sem=rs_send.at[d],
            recv_sem=down_recv.at[d], **on_down)

    def compute(zz):
        part[zz] = block(zz, x, False)
        part[zz] += block(zz, across, False)

        @pl.when((z == 0) & (zz > z))
        def _():
            rs_out[zz] = part[zz].astype(jnp.bfloat16)
            rs_to_up(zz).start()

        @pl.when((z == slow - 1) & (zz < z))
        def _():
            rs_out[zz] = part[zz].astype(jnp.bfloat16)
            rs_to_down(zz).start()

    def relay(k):
        zz = layer(k)
        a_up(zz).wait_recv()
        forward(zz)
        return zz

    part[z] = block(z, x, True)
    if slow > 1:
        second = relay(1)
    if slow > 2:
        @pl.when(near >= 1)
        def _():
            relay(2)

    b_cross_arrival.wait_recv()
    b_relay.start()
    b_relay_arrival.wait_recv()
    part[z] += block(z, across, True)
    if slow > 1:
        compute(second)

    def line(k, carry):
        @pl.when((k != 2) | (near < 1))
        def _():
            relay(k)

        compute(layer(k))
        return carry

    lax.fori_loop(2, slow, line, 0)

    b_half = pltpu.make_async_remote_copy(
        src_ref=b_half_out, dst_ref=b_half_in, send_sem=gb_send.at[0], recv_sem=gb_recv.at[0], **on_chip)
    b_sum = pltpu.make_async_remote_copy(
        src_ref=b_cross_out, dst_ref=b_cross_in, send_sem=gb_send.at[1], recv_sem=gb_recv.at[1], **on_cross)
    b_half_out[...] = acc_b[across, 1 - core].astype(jnp.bfloat16)
    b_half.start()
    b_half.wait_recv()
    b_cross_out[...] = (acc_b[across, core] + b_half_in[...].astype(jnp.float32)).astype(jnp.bfloat16)
    b_sum.start()

    def pass_on(t, carry):
        @pl.when(has_down & (t > 2 * z) & (t < slow + z))
        def _():
            d = t - z
            rs_to_up(d).wait_recv()
            rs_out[d] = (part[d] + rs_up[d].astype(jnp.float32)).astype(jnp.bfloat16)
            rs_to_up(d).start()

        z_back = slow - 1 - z

        @pl.when(has_up & (t > 2 * z_back) & (t < slow + z_back))
        def _():
            d = slow - 1 - (t - z_back)
            rs_to_down(d).wait_recv()
            rs_out[d] = (part[d] + rs_down[d].astype(jnp.float32)).astype(jnp.bfloat16)
            rs_to_down(d).start()

        return carry

    lax.fori_loop(3, 2 * slow - 2, pass_on, 0)

    b_sum.wait_recv()
    to_b = pltpu.make_async_remote_copy(
        src_ref=last_out, dst_ref=last_in, send_sem=gb_send.at[2], recv_sem=gb_recv.at[2], **on_chip)
    to_a = pltpu.make_async_remote_copy(
        src_ref=last_out.at[0], dst_ref=last_in.at[0], send_sem=gb_send.at[2], recv_sem=gb_recv.at[2],
        **on_chip)

    @pl.when(core == 0)
    def _():
        last_out[0] = (acc_b[x, 0] + b_cross_in[...].astype(jnp.float32)).astype(jnp.bfloat16)
        last_out[1] = acc_b[x, 1].astype(jnp.bfloat16)
        to_b.start()

    @pl.when(has_down)
    def _():
        rs_to_up(z).wait_recv()
        part[z] += rs_up[z].astype(jnp.float32)

    @pl.when(has_up)
    def _():
        rs_to_down(z).wait_recv()
        part[z] += rs_down[z].astype(jnp.float32)

    @pl.when(core == 0)
    def _():
        out_ref[0, pl.ds(0, half), :] = part[z]
        to_a.wait_recv()
        out_ref[0, pl.ds(half, half), :] = last_in[0].astype(jnp.float32)
        a_swap.wait_send()
        to_b.wait_send()

    @pl.when(core == 1)
    def _():
        last_out[0] = part[z].astype(jnp.bfloat16)
        to_a.start()
        to_b.wait_recv()
        out_ref[0, pl.ds(0, half), :] = acc_b[x, 0] + last_in[0].astype(jnp.float32)
        out_ref[0, pl.ds(half, half), :] = (
            acc_b[x, 1] + last_in[1].astype(jnp.float32) + b_cross_in[...].astype(jnp.float32))
        b_swap.wait_send()
        to_a.wait_send()

    b_cross.wait_send()
    b_relay.wait_send()
    b_half.wait_send()
    b_sum.wait_send()

    def drain(zz, carry):
        @pl.when(has_up & (zz <= z))
        def _():
            a_up(zz).wait_send()

        @pl.when(has_down & (zz >= z))
        def _():
            a_down(zz).wait_send()

        @pl.when(zz > z)
        def _():
            rs_to_up(zz).wait_send()

        @pl.when(zz < z)
        def _():
            rs_to_down(zz).wait_send()

        return carry

    lax.fori_loop(0, slow, drain, 0)


def solution(mesh):
    n = mesh.shape["blk"]
    fast = 2
    slow = n // fast

    def on_device(patch_rows, subject_ids, logit_scale, logit_bias):
        _, rows, patches, width = patch_rows.shape
        half = rows // 2
        chunk = 48 if rows % 48 == 0 else rows
        bf16, f32 = jnp.bfloat16, jnp.float32
        dma = pltpu.SemaphoreType.DMA
        return pl.pallas_call(
            functools.partial(kernel, n, fast),
            out_shape=jax.ShapeDtypeStruct((1, rows, width), jnp.float32),
            in_specs=[pl.BlockSpec(memory_space=pltpu.SMEM), pl.BlockSpec(memory_space=pltpu.SMEM),
                      pl.BlockSpec(memory_space=pltpu.VMEM), pl.BlockSpec(memory_space=pl.ANY)],
            out_specs=pl.BlockSpec(memory_space=pltpu.VMEM),
            scratch_shapes=[
                pltpu.VMEM((rows // chunk, chunk, patches, width), bf16),
                pltpu.VMEM((2, half, width), bf16),
                pltpu.VMEM((slow, half, width), bf16),
                pltpu.VMEM((fast, 2, half, width), bf16),
                pltpu.VMEM((slow, rows, 1), f32),
                pltpu.VMEM((slow, half, width), f32),
                pltpu.VMEM((fast, 2, half, width), f32),
                pltpu.VMEM((slow, half, width), bf16),
                pltpu.VMEM((slow, half, width), bf16),
                pltpu.VMEM((slow, half, width), bf16),
                pltpu.VMEM((half, width), bf16),
                pltpu.VMEM((half, width), bf16),
                pltpu.VMEM((half, width), bf16),
                pltpu.VMEM((half, width), bf16),
                pltpu.VMEM((2, half, width), bf16),
                pltpu.VMEM((2, half, width), bf16),
                dma((rows // chunk,)), dma, dma, dma((slow,)), dma((slow,)), dma((slow,)),
                dma, dma, dma, dma, dma((slow,)), dma((slow,)), dma((slow,)), dma((3,)), dma((3,)),
            ],
            compiler_params=pltpu.CompilerParams(
                collective_id=0, has_side_effects=True, vmem_limit_bytes=60 * 2**20),
        )(logit_scale, logit_bias, subject_ids.reshape(n, rows), patch_rows)

    return jax.shard_map(
        on_device, mesh=mesh, in_specs=(P("con", "blk", None, None), P(), P(), P()),
        out_specs=P("con", "blk", None), check_vma=False)
```

```python
import functools
import jax
import jax.numpy as jnp
from jax import lax
from jax.experimental import pallas as pl
from jax.experimental.pallas import tpu as pltpu
from jax.sharding import PartitionSpec as P

MESH = pl.DeviceIdType.MESH


def kernel(n, fast, scale_ref, bias_ref, ids_ref, x_ref, out_ref, xbuf, own, a_rows, b_rows,
           ids_col, part, acc_b, rs_out, rs_up, rs_down, b_half_out, b_half_in, b_cross_out,
           b_cross_in, last_out, last_in, in_sem, swap_send, swap_recv, a_recv, up_send, down_send,
           b_cross_send, b_cross_recv, b_relay_send, b_relay_recv, rs_send, up_recv, down_recv,
           gb_send, gb_recv):
    rows, patches, width = x_ref.shape[1:]
    half = rows // 2
    slow = n // fast
    con = lax.axis_index("con")
    pos = lax.axis_index("blk")
    z = pos // fast
    x = pos % fast
    pair = con // 2
    core = con % 2
    partner = con + 1 - 2 * core
    across = x + 1 - 2 * (x % 2)
    group = 16
    steps = xbuf.shape[0]
    chunk = rows // steps
    on_chip = dict(device_id=(pos, partner), device_id_type=MESH)
    on_cross = dict(device_id=(z * fast + across, con), device_id_type=MESH)
    on_up = dict(device_id=(pos + fast, con), device_id_type=MESH)
    on_down = dict(device_id=(pos - fast, con), device_id_type=MESH)
    has_up = z < slow - 1
    has_down = z > 0

    def load(i):
        return pltpu.make_async_copy(
            x_ref.at[0, pl.ds(i * chunk, chunk)], xbuf.at[i], in_sem.at[i])

    for i in range(steps):
        load(i).start()

    barrier = pltpu.get_barrier_semaphore()
    pl.semaphore_signal(barrier, inc=1, **on_chip)
    pl.semaphore_signal(barrier, inc=1, **on_cross)

    @pl.when(has_down)
    def _():
        pl.semaphore_signal(barrier, inc=1, **on_down)

    @pl.when(has_up)
    def _():
        pl.semaphore_signal(barrier, inc=1, **on_up)

    eye = (lax.broadcasted_iota(jnp.int32, (rows, rows), 0)
           == lax.broadcasted_iota(jnp.int32, (rows, rows), 1))

    def column(zz, carry):
        line = ids_ref[pl.ds(zz * fast + x, 1), :].astype(jnp.float32)
        ids_col[zz] = jnp.sum(jnp.where(eye, line, 0.0), axis=1, keepdims=True)
        return carry

    lax.fori_loop(0, slow, column, 0)

    ones = (lax.broadcasted_iota(jnp.int32, (group, group * patches), 1) // patches
            == lax.broadcasted_iota(jnp.int32, (group, group * patches), 0)).astype(jnp.bfloat16)
    for i in range(steps):
        load(i).wait()
        for g in range(chunk // group):
            tile = xbuf[i, pl.ds(g * group, group)].reshape(group * patches, width)
            pooled = jnp.dot(ones, tile, preferred_element_type=jnp.float32) * (1.0 / patches)
            norm = lax.rsqrt(jnp.sum(pooled * pooled, axis=1, keepdims=True) + 1e-6)
            at = i * chunk + g * group
            own[at // half, pl.ds(at % half, group), :] = (pooled * norm).astype(jnp.bfloat16)

    pl.semaphore_wait(barrier, 2 + jnp.where(has_down, 1, 0) + jnp.where(has_up, 1, 0))

    a_swap = pltpu.make_async_remote_copy(
        src_ref=own.at[1], dst_ref=a_rows.at[z], send_sem=swap_send, recv_sem=a_recv.at[z], **on_chip)
    b_swap = pltpu.make_async_remote_copy(
        src_ref=own, dst_ref=b_rows.at[x], send_sem=swap_send, recv_sem=swap_recv, **on_chip)
    b_cross = pltpu.make_async_remote_copy(
        src_ref=b_rows.at[x, core], dst_ref=b_rows.at[x, core], send_sem=b_cross_send,
        recv_sem=b_cross_recv, **on_cross)
    b_cross_arrival = pltpu.make_async_remote_copy(
        src_ref=b_rows.at[across, core], dst_ref=b_rows.at[across, core], send_sem=b_cross_send,
        recv_sem=b_cross_recv, **on_cross)
    b_relay = pltpu.make_async_remote_copy(
        src_ref=b_rows.at[across, core], dst_ref=b_rows.at[across, core], send_sem=b_relay_send,
        recv_sem=b_relay_recv, **on_chip)
    b_relay_arrival = pltpu.make_async_remote_copy(
        src_ref=b_rows.at[across, 1 - core], dst_ref=b_rows.at[across, 1 - core],
        send_sem=b_relay_send, recv_sem=b_relay_recv, **on_chip)

    def a_up(zz):
        return pltpu.make_async_remote_copy(
            src_ref=a_rows.at[zz], dst_ref=a_rows.at[zz], send_sem=up_send.at[zz],
            recv_sem=a_recv.at[zz], **on_up)

    def a_down(zz):
        return pltpu.make_async_remote_copy(
            src_ref=a_rows.at[zz], dst_ref=a_rows.at[zz], send_sem=down_send.at[zz],
            recv_sem=a_recv.at[zz], **on_down)

    def forward(zz):
        @pl.when(has_up & (zz <= z))
        def _():
            a_up(zz).start()

        @pl.when(has_down & (zz >= z))
        def _():
            a_down(zz).start()

    @pl.when(core == 0)
    def _():
        a_rows[z] = own[0]
        a_swap.start()
        forward(z)
        b_swap.wait_recv()
        b_cross.start()

    @pl.when(core == 1)
    def _():
        b_rows[x] = own[...]
        b_swap.start()
        b_cross.start()
        a_swap.wait_recv()
        forward(z)

    near = jnp.minimum(z, slow - 1 - z)
    far_sign = jnp.where(z < slow - 1 - z, 1, -1)

    def layer(k):
        both = ((k + 1) // 2) * jnp.where(k % 2 == 1, 1, -1)
        return z + jnp.where(k <= 2 * near, both, far_sign * (k - near))

    scale = scale_ref[pair]
    bias = bias_ref[pair]

    def block(zz, xx, first):
        rows_a = a_rows[zz]
        rows_b = b_rows[xx].reshape(rows, width)
        dots = lax.dot_general(rows_a, rows_b, (((1,), (1,)), ((), ())),
                               preferred_element_type=jnp.float32)
        logits = scale * dots + bias
        labels = ids_col[zz, pl.ds(pl.multiple_of(core * half, 16), half), :]
        same = labels == ids_ref[pl.ds(z * fast + xx, 1), :].astype(jnp.float32)
        sign = jnp.where(same, 1.0, -1.0)
        coeff = ((-scale * sign) / (1.0 + jnp.exp(sign * logits))).astype(jnp.bfloat16)
        grad_b = lax.dot_general(coeff, rows_a, (((0,), (0,)), ((), ())),
                                 preferred_element_type=jnp.float32).reshape(2, half, width)
        if first:
            acc_b[xx] = grad_b
        else:
            acc_b[xx] += grad_b
        return jnp.dot(coeff, rows_b, preferred_element_type=jnp.float32)

    def rs_to_up(d):
        return pltpu.make_async_remote_copy(
            src_ref=rs_out.at[d], dst_ref=rs_up.at[d], send_sem=rs_send.at[d],
            recv_sem=up_recv.at[d], **on_up)

    def rs_to_down(d):
        return pltpu.make_async_remote_copy(
            src_ref=rs_out.at[d], dst_ref=rs_down.at[d], send_sem=rs_send.at[d],
            recv_sem=down_recv.at[d], **on_down)

    def compute(zz):
        part[zz] = block(zz, x, False)
        part[zz] += block(zz, across, False)

        @pl.when((z == 0) & (zz > z))
        def _():
            rs_out[zz] = part[zz].astype(jnp.bfloat16)
            rs_to_up(zz).start()

        @pl.when((z == slow - 1) & (zz < z))
        def _():
            rs_out[zz] = part[zz].astype(jnp.bfloat16)
            rs_to_down(zz).start()

    def relay(k):
        zz = layer(k)
        a_up(zz).wait_recv()
        forward(zz)
        return zz

    part[z] = block(z, x, True)
    if slow > 1:
        second = relay(1)
    if slow > 2:
        @pl.when(near >= 1)
        def _():
            relay(2)

    b_cross_arrival.wait_recv()
    b_relay.start()
    b_relay_arrival.wait_recv()
    part[z] += block(z, across, True)
    if slow > 1:
        compute(second)

    def line(k, carry):
        @pl.when((k != 2) | (near < 1))
        def _():
            relay(k)

        compute(layer(k))
        return carry

    lax.fori_loop(2, slow, line, 0)

    b_half = pltpu.make_async_remote_copy(
        src_ref=b_half_out, dst_ref=b_half_in, send_sem=gb_send.at[0], recv_sem=gb_recv.at[0], **on_chip)
    b_sum = pltpu.make_async_remote_copy(
        src_ref=b_cross_out, dst_ref=b_cross_in, send_sem=gb_send.at[1], recv_sem=gb_recv.at[1], **on_cross)
    b_half_out[...] = acc_b[across, 1 - core].astype(jnp.bfloat16)
    b_half.start()
    b_half.wait_recv()
    b_cross_out[...] = (acc_b[across, core] + b_half_in[...].astype(jnp.float32)).astype(jnp.bfloat16)
    b_sum.start()

    def pass_on(t, carry):
        @pl.when(has_down & (t > 2 * z) & (t < slow + z))
        def _():
            d = t - z
            rs_to_up(d).wait_recv()
            rs_out[d] = (part[d] + rs_up[d].astype(jnp.float32)).astype(jnp.bfloat16)
            rs_to_up(d).start()

        z_back = slow - 1 - z

        @pl.when(has_up & (t > 2 * z_back) & (t < slow + z_back))
        def _():
            d = slow - 1 - (t - z_back)
            rs_to_down(d).wait_recv()
            rs_out[d] = (part[d] + rs_down[d].astype(jnp.float32)).astype(jnp.bfloat16)
            rs_to_down(d).start()

        return carry

    lax.fori_loop(3, 2 * slow - 2, pass_on, 0)

    b_sum.wait_recv()
    to_b = pltpu.make_async_remote_copy(
        src_ref=last_out, dst_ref=last_in, send_sem=gb_send.at[2], recv_sem=gb_recv.at[2], **on_chip)
    to_a = pltpu.make_async_remote_copy(
        src_ref=last_out.at[0], dst_ref=last_in.at[0], send_sem=gb_send.at[2], recv_sem=gb_recv.at[2],
        **on_chip)

    @pl.when(core == 0)
    def _():
        last_out[0] = (acc_b[x, 0] + b_cross_in[...].astype(jnp.float32)).astype(jnp.bfloat16)
        last_out[1] = acc_b[x, 1].astype(jnp.bfloat16)
        to_b.start()

    @pl.when(has_down)
    def _():
        rs_to_up(z).wait_recv()
        part[z] += rs_up[z].astype(jnp.float32)

    @pl.when(has_up)
    def _():
        rs_to_down(z).wait_recv()
        part[z] += rs_down[z].astype(jnp.float32)

    @pl.when(core == 0)
    def _():
        out_ref[0, pl.ds(0, half), :] = part[z]
        to_a.wait_recv()
        out_ref[0, pl.ds(half, half), :] = last_in[0].astype(jnp.float32)
        a_swap.wait_send()
        to_b.wait_send()

    @pl.when(core == 1)
    def _():
        last_out[0] = part[z].astype(jnp.bfloat16)
        to_a.start()
        to_b.wait_recv()
        out_ref[0, pl.ds(0, half), :] = acc_b[x, 0] + last_in[0].astype(jnp.float32)
        out_ref[0, pl.ds(half, half), :] = (
            acc_b[x, 1] + last_in[1].astype(jnp.float32) + b_cross_in[...].astype(jnp.float32))
        b_swap.wait_send()
        to_a.wait_send()

    b_cross.wait_send()
    b_relay.wait_send()
    b_half.wait_send()
    b_sum.wait_send()

    def drain(zz, carry):
        @pl.when(has_up & (zz <= z))
        def _():
            a_up(zz).wait_send()

        @pl.when(has_down & (zz >= z))
        def _():
            a_down(zz).wait_send()

        @pl.when(zz > z)
        def _():
            rs_to_up(zz).wait_send()

        @pl.when(zz < z)
        def _():
            rs_to_down(zz).wait_send()

        return carry

    lax.fori_loop(0, slow, drain, 0)


def solution(mesh):
    n = mesh.shape["blk"]
    fast = 2
    slow = n // fast

    def on_device(patch_rows, subject_ids, logit_scale, logit_bias):
        _, rows, patches, width = patch_rows.shape
        half = rows // 2
        chunk = 48 if rows % 48 == 0 else rows
        bf16, f32 = jnp.bfloat16, jnp.float32
        dma = pltpu.SemaphoreType.DMA
        need = 2 * rows * patches * width + half * width * (12 * slow + 12 * fast + 28)
        need += slow * rows * 512
        return pl.pallas_call(
            functools.partial(kernel, n, fast),
            out_shape=jax.ShapeDtypeStruct((1, rows, width), jnp.float32),
            in_specs=[pl.BlockSpec(memory_space=pltpu.SMEM), pl.BlockSpec(memory_space=pltpu.SMEM),
                      pl.BlockSpec(memory_space=pltpu.VMEM), pl.BlockSpec(memory_space=pl.ANY)],
            out_specs=pl.BlockSpec(memory_space=pltpu.VMEM),
            scratch_shapes=[
                pltpu.VMEM((rows // chunk, chunk, patches, width), bf16),
                pltpu.VMEM((2, half, width), bf16),
                pltpu.VMEM((slow, half, width), bf16),
                pltpu.VMEM((fast, 2, half, width), bf16),
                pltpu.VMEM((slow, rows, 1), f32),
                pltpu.VMEM((slow, half, width), f32),
                pltpu.VMEM((fast, 2, half, width), f32),
                pltpu.VMEM((slow, half, width), bf16),
                pltpu.VMEM((slow, half, width), bf16),
                pltpu.VMEM((slow, half, width), bf16),
                pltpu.VMEM((half, width), bf16),
                pltpu.VMEM((half, width), bf16),
                pltpu.VMEM((half, width), bf16),
                pltpu.VMEM((half, width), bf16),
                pltpu.VMEM((2, half, width), bf16),
                pltpu.VMEM((2, half, width), bf16),
                dma((rows // chunk,)), dma, dma, dma((slow,)), dma((slow,)), dma((slow,)),
                dma, dma, dma, dma, dma((slow,)), dma((slow,)), dma((slow,)), dma((3,)), dma((3,)),
            ],
            compiler_params=pltpu.CompilerParams(
                collective_id=0, has_side_effects=True, vmem_limit_bytes=min(need + 12 * 2**20, 60 * 2**20)),
        )(logit_scale, logit_bias, subject_ids.reshape(n, rows), patch_rows)

    return jax.shard_map(
        on_device, mesh=mesh, in_specs=(P("con", "blk", None, None), P(), P(), P()),
        out_specs=P("con", "blk", None), check_vma=False)
```
